256 devices in a mesh: replica: 32 (over x, z), shard: 8 (over y, core).
Axes of the slice: x: 4, y: 4, z: 8, core: 2. Of those that a mesh axis runs over, the one named last changes fastest.
Arguments:
- grads: bfloat16 [32, 8192, 2048], P('replica', 'shard'), may hold values from -64 to 64
- errors: bfloat16 [32, 8192, 2048], P('replica', 'shard'), may hold values from -4 to 4
- q_prev: bfloat16 [32, 2048], P(None, 'shard'), may hold values from -6 to 6
- momentum: float32 [8192, 2048], P('shard', 'replica'), may hold values from -1.2 to 1.2
Outputs:
- new_errors: bfloat16 [32, 8192, 2048], P('replica', 'shard')
- new_momentum: float32 [8192, 2048], P('shard', 'replica')
- q_next: float32 [32, 2048], P(None, 'shard')
The draws below stay inside these ranges and needn't reach their ends.
All inputs are finite; a program needn't handle non-finite values.
Results may differ from the reference program's by a relative error of at most 0.012.
Values may be sent and summed in bfloat16 or wider, within the bound.
A program may use at most 64 MiB of HBM per device.

```python
import math
import jax
import jax.numpy as jnp
from jax import lax

D = 2048
ROWS = 8192
R = 32
N_REPLICA = 32


def signed_vector(key, shape):
    keys = jax.random.split(key, 2)
    magnitude = jax.random.uniform(keys[0], shape, jnp.float32, 0.5, 1.5)
    signs = jnp.where(jax.random.bernoulli(keys[1], 0.5, shape), 1.0, -1.0).astype(jnp.float32)
    return magnitude * signs


def draw_grads(key, part):
    keys = jax.random.split(key, 6)
    row_scale = jnp.exp(jax.random.uniform(keys[0], (1, ROWS, 1), jnp.float32, math.log(0.3), math.log(3.0)))
    col_scale = jnp.exp(jax.random.uniform(keys[1], (1, 1, D), jnp.float32, math.log(0.4), math.log(4.0)))
    values = jnp.clip(jax.random.normal(keys[2], (N_REPLICA, ROWS, D), jnp.float32), -6.0, 6.0)
    row_vector = signed_vector(keys[4], (1, ROWS, 1))
    col_vector = signed_vector(keys[5], (1, 1, D))
    replica_ids = jnp.arange(N_REPLICA, dtype=jnp.int32)
    upper_sign = (1 - 2 * (replica_ids // max(N_REPLICA // 4, 1) % 2)).astype(jnp.float32)
    lower_sign = (1 - 2 * (replica_ids % 2)).astype(jnp.float32)
    weight = (0.5 + 0.6 * upper_sign + 0.3 * lower_sign).reshape(N_REPLICA, 1, 1)
    values = values * row_scale * col_scale + weight * row_vector * col_vector
    return jnp.clip(values, -64.0, 64.0).astype(jnp.bfloat16)


def shard_levels(own_key, extent, cuts, smallest, high):
    def one(axis_at, shards_of):
        steps = jax.random.uniform(jax.random.fold_in(jax.random.fold_in(own_key, 6), axis_at), (shards_of,), jnp.float32, smallest / len(cuts), high / len(cuts))
        return jnp.repeat(jnp.exp(steps), extent[axis_at] // shards_of).reshape((-1,) + (1,) * (len(extent) - axis_at - 1))

    level = one(*cuts[0])
    for cut in cuts[1:]:
        level = level * one(*cut)
    return level


def gaussian(own_key, dims, spread, limit, cuts=(), held_as=jnp.bfloat16):
    result = jax.random.normal(own_key, dims, jnp.float32) * spread
    if len(cuts) > 0:
        result = shard_levels(own_key, dims, cuts, -0.22, 0.18) * result
    return jnp.clip(result, min=-limit, max=limit).astype(held_as)


def setup_inputs(seed: int = 0) -> dict:
    arg_keys = jax.random.split(jax.random.key(seed), 5)
    grads = draw_grads(jax.random.fold_in(arg_keys[4], 71), 0)
    errors = gaussian(arg_keys[1], (N_REPLICA, ROWS, D), 0.5, 4.0, ((0, 32), (1, 8)))
    q_prev = gaussian(arg_keys[2], (R, D), 1.0, 6.0, ((1, 8),))
    momentum = gaussian(arg_keys[3], (ROWS, D), 0.2, 1.2, ((0, 8), (1, 32)), jnp.float32)
    return dict(grads=grads, errors=errors, q_prev=q_prev, momentum=momentum)


def merged_of(grads, errors, index):
    return grads[index].astype(jnp.float32) + errors[index].astype(jnp.float32)

def reference(grads, errors, q_prev, momentum):
    highest = lax.Precision.HIGHEST
    basis_rows = q_prev.astype(jnp.float32)
    replica_ids = jnp.arange(N_REPLICA, dtype=jnp.int32)

    def add_left(running, index):
        merged = merged_of(grads, errors, index)
        return (running + jnp.dot(merged, basis_rows.T, precision=highest), None)
    factor, _ = lax.scan(add_left, jnp.zeros((ROWS, R), jnp.float32), replica_ids)
    gram_matrix = jnp.dot(factor.T, factor, precision=highest)
    lower_factor = jnp.linalg.cholesky(gram_matrix)
    ortho = jax.scipy.linalg.solve_triangular(lower_factor, factor.T, lower=True).T

    def add_right(running, index):
        merged = merged_of(grads, errors, index)
        return (running + jnp.dot(ortho.T, merged, precision=highest), None)
    right_sum, _ = lax.scan(add_right, jnp.zeros((R, D), jnp.float32), replica_ids)
    q_next = right_sum / N_REPLICA
    approx = jnp.dot(ortho, q_next, precision=highest)

    def residue(index):
        return (merged_of(grads, errors, index) - approx).astype(jnp.bfloat16)
    new_errors = lax.map(residue, replica_ids)
    new_momentum = 0.9 * momentum + approx
    return (new_errors, new_momentum, q_next)
```

```python
import functools

import jax
import jax.numpy as jnp
from jax import lax
from jax.experimental import pallas as pl
from jax.experimental.pallas import tpu as pltpu
from jax.sharding import PartitionSpec as P

MESH = pl.DeviceIdType.MESH
NX, NZ, NS = 4, 8, 8
NM = NX * NS
ROWS, COLS, R = 1024, 2048, 32
CH = ROWS // NX
F32, BF16 = jnp.float32, jnp.bfloat16
HIGHEST = lax.Precision.HIGHEST


def dot(a, b, dims, precision=None):
    return lax.dot_general(
        a, b, (dims, ((), ())), precision=precision, preferred_element_type=F32
    )


def wait_bytes(ref, sem):
    pltpu.make_async_copy(ref, ref, sem).wait()


def inverse_factor(gram):
    row = lax.broadcasted_iota(jnp.int32, (R, 128), 0)
    lane = lax.broadcasted_iota(jnp.int32, (R, 128), 1)
    eye = jnp.where(row == lane, 1.0, 0.0).astype(F32)
    work = eye + jnp.concatenate(
        [jnp.zeros((R, R), F32), gram, jnp.zeros((R, 128 - 2 * R), F32)], axis=1
    )
    pivots = jnp.ones((R, 128), F32)
    for j in range(R):
        column = jnp.broadcast_to(work[:, R + j : R + j + 1], (R, 128))
        pivot = column[j : j + 1, :]
        pivots = jnp.where(row == j, pivot, pivots)
        scaled = work[j : j + 1, :] * (1.0 / pivot)
        work = work - jnp.where(row > j, column, 0.0) * scaled
    return work[:, :R] * lax.rsqrt(pivots)[:, :R]


def exchange_kernel(
    g_hbm,
    e_hbm,
    q_ref,
    ohl_ref,
    qn_ref,
    qsel_ref,
    gv,
    ev,
    qb,
    xs,
    xr,
    zb,
    pt,
    gb,
    st,
    rt,
    tz,
    qp,
    load_sem,
    send_sem,
    recv_sem,
):
    replica = lax.axis_index("replica")
    s = lax.axis_index("shard")
    x, z = replica // NZ, lax.rem(replica, NZ)
    m = x * NS + s

    def shard_peer(i):
        return (replica, lax.rem(s + i, NS))

    def x_peer(i):
        return (lax.rem(x + i, NX) * NZ + z, s)

    def z_peer(i):
        return (x * NZ + lax.rem(z + i, NZ), s)

    def m_device(p):
        return ((p // NS) * NZ + z, lax.rem(p, NS))

    def send(src, dst, at, device):
        pltpu.make_async_remote_copy(
            src,
            dst,
            send_sem.at[at],
            recv_sem.at[at],
            device_id=device,
            device_id_type=MESH,
        ).start()

    loads = []
    for i in range(1, NX + 1):
        rows = pl.ds(pl.multiple_of(lax.rem(x + i, NX) * CH, CH), CH)
        pair = [
            pltpu.make_async_copy(src.at[rows], dst.at[rows], load_sem.at[2 * (i - 1) + k])
            for k, (src, dst) in enumerate(((g_hbm, gv), (e_hbm, ev)))
        ]
        for copy in pair:
            copy.start()
        loads.append(pair)

    barrier = pltpu.get_barrier_semaphore()

    def greet(i, carry):
        pl.semaphore_signal(
            barrier, inc=1, device_id=m_device(lax.rem(m + i, NM)), device_id_type=MESH
        )
        return carry

    lax.fori_loop(1, NM, greet, 0)
    for i in range(1, NZ):
        pl.semaphore_signal(barrier, inc=1, device_id=z_peer(i), device_id_type=MESH)
    pl.semaphore_wait(barrier, NM - 1 + NZ - 1)

    for i in range(1, NS):
        send(q_ref, qb.at[s], 0, shard_peer(i))
    qb[s] = q_ref[...]
    wait_bytes(qb.at[pl.ds(0, NS - 1)], recv_sem.at[0])

    own = None
    for i in range(1, NX + 1):
        chunk = lax.rem(x + i, NX)
        rows = pl.ds(pl.multiple_of(chunk * CH, CH), CH)
        for copy in loads[i - 1]:
            copy.wait()
        total = jnp.zeros((R, CH), F32)
        for k in range(NS):
            columns = pl.ds(k * 256, 256)
            total += dot(qb[k], gv[rows, columns], ((1,), (1,)))
            total += dot(qb[k], ev[rows, columns], ((1,), (1,)))
        if i < NX:
            xs[i - 1] = total.astype(BF16)
            send(xs.at[i - 1], xr.at[x], 1, x_peer(i))
        else:
            xr[x] = total.astype(BF16)
    wait_bytes(xr.at[pl.ds(0, NX - 1)], recv_sem.at[1])
    total = xr[0].astype(F32)
    for k in range(1, NX):
        total += xr[k].astype(F32)
    zb[z] = total.astype(BF16)
    for i in range(1, NZ):
        send(zb.at[z], zb.at[z], 2, z_peer(i))
    wait_bytes(zb.at[pl.ds(0, NZ - 1)], recv_sem.at[2])
    total = zb[0].astype(F32)
    for k in range(1, NZ):
        total += zb[k].astype(F32)
    pt[x] = total.astype(BF16)
    for i in range(1, NX):
        send(pt.at[x], pt.at[x], 3, x_peer(i))
    wait_bytes(pt.at[pl.ds(0, NX - 1)], recv_sem.at[3])

    gram = jnp.zeros((R, R), F32)
    for c in range(NX):
        gram += dot(pt[c], pt[c], ((1,), (1,)))
    gb[s] = jnp.concatenate([gram[8 * k : 8 * k + 8] for k in range(4)], axis=1)
    for i in range(1, NS):
        send(gb.at[s], gb.at[s], 4, shard_peer(i))

    low = lax.broadcasted_iota(jnp.int32, (16, 128), 1) < 64

    def right_block(i, carry):
        block = lax.rem(m // 4 + i, 8)
        columns = pl.ds(pl.multiple_of(block * 256, 256), 256)
        term = jnp.zeros((R, 256), F32)
        for c in range(NX):
            rows = pl.ds(c * CH, CH)
            term += dot(pt[c], gv[rows, columns], ((1,), (0,)))
            term += dot(pt[c], ev[rows, columns], ((1,), (0,)))
        for t in range(2):
            top = term[:16, 128 * t : 128 * t + 128]
            bottom = term[16:, 128 * t : 128 * t + 128]
            for h in range(2):
                p = block * 4 + 2 * t + h
                if h == 0:
                    piece = jnp.where(low, top, pltpu.roll(bottom, 64, 1))
                else:
                    piece = jnp.where(low, pltpu.roll(top, 64, 1), bottom)
                st[p] = piece

                @pl.when(p != m)
                def _():
                    send(st.at[p], rt.at[m], 5, m_device(p))

        return carry

    lax.fori_loop(1, 9, right_block, 0)
    rt[m] = st[m]

    wait_bytes(gb.at[pl.ds(0, NS - 1)], recv_sem.at[4])
    packed = gb[0]
    for k in range(1, NS):
        packed += gb[k]
    gram = jnp.concatenate([packed[:, R * k : R * k + R] for k in range(4)], axis=0)
    inverse = inverse_factor(gram)

    wait_bytes(rt.at[pl.ds(0, NM - 1)], recv_sem.at[5])
    piece = rt[0]
    for k in range(1, NM):
        piece += rt[k]
    tz[z] = piece
    for i in range(1, NZ):
        send(tz.at[z], tz.at[z], 6, z_peer(i))

    for c in range(NX):
        ortho = dot(pt[c].astype(F32), inverse, ((0,), (1,)), HIGHEST)
        high = ortho.astype(BF16)
        rest = (ortho - high.astype(F32)).astype(BF16)
        ohl_ref[pl.ds(c * CH, CH), :] = jnp.concatenate([high, rest], axis=1)

    wait_bytes(tz.at[pl.ds(0, NZ - 1)], recv_sem.at[6])
    piece = tz[0]
    for k in range(1, NZ):
        piece += tz[k]
    term = jnp.concatenate([piece, pltpu.roll(piece, 64, 1)], axis=0)
    right = dot(inverse, term, ((1,), (0,)), HIGHEST) * (1.0 / 32.0)
    qp[m] = jnp.where(low, right[:16], pltpu.roll(right[16:], 64, 1)).astype(BF16)

    def gather(i, carry):
        send(qp.at[m], qp.at[m], 7, m_device(lax.rem(m + i, NM)))
        return carry

    lax.fori_loop(1, NM, gather, 0)
    wait_bytes(qp.at[pl.ds(0, NM - 1)], recv_sem.at[7])
    for t in range(NM // 2):
        first, second = qp[2 * t].astype(F32), qp[2 * t + 1].astype(F32)
        columns = pl.ds(128 * t, 128)
        qn_ref[:16, columns] = jnp.where(low, first, pltpu.roll(second, 64, 1)).astype(BF16)
        qn_ref[16:, columns] = jnp.where(low, pltpu.roll(first, 64, 1), second).astype(BF16)
    mine = qp[replica].astype(F32)
    qsel_ref[:16] = mine.astype(BF16)
    qsel_ref[16:] = pltpu.roll(mine, 64, 1).astype(BF16)

    for ref, at in (
        (qb.at[pl.ds(0, NS - 1)], 0),
        (xr.at[pl.ds(0, NX - 1)], 1),
        (zb.at[pl.ds(0, NZ - 1)], 2),
        (pt.at[pl.ds(0, NX - 1)], 3),
        (gb.at[pl.ds(0, NS - 1)], 4),
        (rt.at[pl.ds(0, NM - 1)], 5),
        (tz.at[pl.ds(0, NZ - 1)], 6),
        (qp.at[pl.ds(0, NM - 1)], 7),
    ):
        wait_bytes(ref, send_sem.at[at])


def residual_kernel(g_ref, e_ref, ohl_ref, qn_ref, qsel_ref, mom_ref, err_ref, new_ref, q_ref):
    s = lax.axis_index("shard")
    q = qn_ref[...]
    ohl = ohl_ref[...]
    approx = dot(ohl, jnp.concatenate([q, q], axis=0), ((1,), (0,)))
    merged = g_ref[...].astype(F32) + e_ref[...].astype(F32)
    err_ref[...] = (merged - approx).astype(BF16)
    chosen = qsel_ref[...]
    block = dot(ohl, jnp.concatenate([chosen, chosen], axis=0), ((1,), (0,)))
    new_ref[...] = 0.9 * mom_ref[...] + block[:, :64]
    q_ref[...] = qn_ref[:, pl.ds(pl.multiple_of(s * 256, 256), 256)].astype(F32)


def shards(grads, errors, q_prev, momentum):
    g, e = grads[0], errors[0]
    vmem = pl.BlockSpec(memory_space=pltpu.VMEM)
    hbm = pl.BlockSpec(memory_space=pltpu.HBM)
    ohl, qn, qsel = pl.pallas_call(
        exchange_kernel,
        out_shape=(
            jax.ShapeDtypeStruct((ROWS, 2 * R), BF16),
            jax.ShapeDtypeStruct((R, COLS), BF16),
            jax.ShapeDtypeStruct((R, 128), BF16),
        ),
        in_specs=[hbm, hbm, vmem],
        out_specs=(vmem, vmem, vmem),
        scratch_shapes=[
            pltpu.VMEM((ROWS, COLS), BF16),
            pltpu.VMEM((ROWS, COLS), BF16),
            pltpu.VMEM((NS, R, 256), BF16),
            pltpu.VMEM((NX - 1, R, CH), BF16),
            pltpu.VMEM((NX, R, CH), BF16),
            pltpu.VMEM((NZ, R, CH), BF16),
            pltpu.VMEM((NX, R, CH), BF16),
            pltpu.VMEM((NS, 8, 128), F32),
            pltpu.VMEM((NM, 16, 128), F32),
            pltpu.VMEM((NM, 16, 128), F32),
            pltpu.VMEM((NZ, 16, 128), F32),
            pltpu.VMEM((NM, 16, 128), BF16),
            pltpu.SemaphoreType.DMA((2 * NX,)),
            pltpu.SemaphoreType.DMA((8,)),
            pltpu.SemaphoreType.DMA((8,)),
        ],
        compiler_params=pltpu.CompilerParams(
            collective_id=0, has_side_effects=True, vmem_limit_bytes=40 << 20
        ),
    )(g, e, q_prev)
    tile = 128
    new_errors, new_momentum, q_next = pl.pallas_call(
        residual_kernel,
        grid=(ROWS // tile,),
        out_shape=(
            jax.ShapeDtypeStruct((ROWS, COLS), BF16),
            jax.ShapeDtypeStruct((ROWS, 64), F32),
            jax.ShapeDtypeStruct((R, 256), F32),
        ),
        in_specs=[
            pl.BlockSpec((tile, COLS), lambda i: (i, 0)),
            pl.BlockSpec((tile, COLS), lambda i: (i, 0)),
            pl.BlockSpec((tile, 2 * R), lambda i: (i, 0)),
            pl.BlockSpec((R, COLS), lambda i: (0, 0)),
            pl.BlockSpec((R, 128), lambda i: (0, 0)),
            pl.BlockSpec((tile, 64), lambda i: (i, 0)),
        ],
        out_specs=(
            pl.BlockSpec((tile, COLS), lambda i: (i, 0)),
            pl.BlockSpec((tile, 64), lambda i: (i, 0)),
            pl.BlockSpec((R, 256), lambda i: (0, 0)),
        ),
        compiler_params=pltpu.CompilerParams(vmem_limit_bytes=40 << 20),
    )(g, e, ohl, qn, qsel, momentum)
    return (new_errors[None], new_momentum, q_next)


def solution(mesh):
    return jax.shard_map(
        shards,
        mesh=mesh,
        in_specs=(
            P("replica", "shard", None),
            P("replica", "shard", None),
            P(None, "shard"),
            P("shard", "replica"),
        ),
        out_specs=(P("replica", "shard", None), P("shard", "replica"), P(None, "shard")),
        check_vma=False,
    )
```

```python
import functools

import jax
import jax.numpy as jnp
from jax import lax
from jax.experimental import pallas as pl
from jax.experimental.pallas import tpu as pltpu
from jax.sharding import PartitionSpec as P

MESH = pl.DeviceIdType.MESH
NX, NZ, NS = 4, 8, 8
NM = NX * NS
ROWS, COLS, R = 1024, 2048, 32
CH = ROWS // NX
F32, BF16 = jnp.float32, jnp.bfloat16
TILE = 128
HIGHEST = lax.Precision.HIGHEST


def dot(a, b, dims, precision=None):
    return lax.dot_general(
        a, b, (dims, ((), ())), precision=precision, preferred_element_type=F32
    )


def wait_bytes(ref, sem):
    pltpu.make_async_copy(ref, ref, sem).wait()


def inverse_factor(gram):
    row = lax.broadcasted_iota(jnp.int32, (R, 128), 0)
    lane = lax.broadcasted_iota(jnp.int32, (R, 128), 1)
    eye = jnp.where(row == lane, 1.0, 0.0).astype(F32)
    work = eye + jnp.concatenate(
        [jnp.zeros((R, R), F32), gram, jnp.zeros((R, 128 - 2 * R), F32)], axis=1
    )
    pivots = jnp.ones((R, 128), F32)
    for j in range(R):
        column = jnp.broadcast_to(work[:, R + j : R + j + 1], (R, 128))
        pivot = column[j : j + 1, :]
        pivots = jnp.where(row == j, pivot, pivots)
        scaled = work[j : j + 1, :] * (1.0 / pivot)
        work = work - jnp.where(row > j, column, 0.0) * scaled
    return work[:, :R] * lax.rsqrt(pivots)[:, :R]


def exchange_kernel(
    g_hbm,
    e_hbm,
    q_hbm,
    merged_ref,
    ohl_ref,
    qn_ref,
    qsel_ref,
    gv,
    ev,
    qb,
    xs,
    xr,
    zb,
    pt,
    gb,
    st,
    rt,
    tz,
    qp,
    load_sem,
    send_sem,
    recv_sem,
):
    replica = lax.axis_index("replica")
    s = lax.axis_index("shard")
    x, z = replica // NZ, lax.rem(replica, NZ)
    m = x * NS + s

    def shard_peer(i):
        return (replica, lax.rem(s + i, NS))

    def x_peer(i):
        return (lax.rem(x + i, NX) * NZ + z, s)

    def z_peer(i):
        return (x * NZ + lax.rem(z + i, NZ), s)

    def m_device(p):
        return ((p // NS) * NZ + z, lax.rem(p, NS))

    def send(src, dst, at, device):
        pltpu.make_async_remote_copy(
            src,
            dst,
            send_sem.at[at],
            recv_sem.at[at],
            device_id=device,
            device_id_type=MESH,
        ).start()

    q_load = pltpu.make_async_copy(q_hbm, qb.at[s], load_sem.at[2 * NX])
    q_load.start()
    loads = []
    for i in range(1, NX + 1):
        rows = pl.ds(pl.multiple_of(lax.rem(x + i, NX) * CH, CH), CH)
        pair = [
            pltpu.make_async_copy(src.at[rows], dst.at[rows], load_sem.at[2 * (i - 1) + k])
            for k, (src, dst) in enumerate(((g_hbm, gv), (e_hbm, ev)))
        ]
        for copy in pair:
            copy.start()
        loads.append(pair)

    barrier = pltpu.get_barrier_semaphore()

    def greet(i, carry):
        pl.semaphore_signal(
            barrier, inc=1, device_id=m_device(lax.rem(m + i, NM)), device_id_type=MESH
        )
        return carry

    lax.fori_loop(1, NM, greet, 0)
    for i in range(1, NZ):
        pl.semaphore_signal(barrier, inc=1, device_id=z_peer(i), device_id_type=MESH)
    pl.semaphore_wait(barrier, NM - 1 + NZ - 1)

    q_load.wait()
    for i in range(1, NS):
        send(qb.at[s], qb.at[s], 0, shard_peer(i))
    wait_bytes(qb.at[pl.ds(0, NS - 1)], recv_sem.at[0])

    own = None
    for i in range(1, NX + 1):
        chunk = lax.rem(x + i, NX)
        rows = pl.ds(pl.multiple_of(chunk * CH, CH), CH)
        for copy in loads[i - 1]:
            copy.wait()
        total = jnp.zeros((R, CH), F32)
        for k in range(NS):
            columns = pl.ds(k * 256, 256)
            total += dot(qb[k], gv[rows, columns], ((1,), (1,)))
            total += dot(qb[k], ev[rows, columns], ((1,), (1,)))
        if i < NX:
            xs[i - 1] = total.astype(BF16)
            send(xs.at[i - 1], xr.at[x], 1, x_peer(i))
        else:
            xr[x] = total.astype(BF16)
    wait_bytes(xr.at[pl.ds(0, NX - 1)], recv_sem.at[1])
    total = xr[0].astype(F32)
    for k in range(1, NX):
        total += xr[k].astype(F32)
    zb[z] = total.astype(BF16)
    for i in range(1, NZ):
        send(zb.at[z], zb.at[z], 2, z_peer(i))
    wait_bytes(zb.at[pl.ds(0, NZ - 1)], recv_sem.at[2])
    total = zb[0].astype(F32)
    for k in range(1, NZ):
        total += zb[k].astype(F32)
    pt[x] = total.astype(BF16)
    for i in range(1, NX):
        send(pt.at[x], pt.at[x], 3, x_peer(i))
    wait_bytes(pt.at[pl.ds(0, NX - 1)], recv_sem.at[3])

    gram = jnp.zeros((R, R), F32)
    for c in range(NX):
        gram += dot(pt[c], pt[c], ((1,), (1,)))
    gb[s] = jnp.concatenate([gram[8 * k : 8 * k + 8] for k in range(4)], axis=1)
    for i in range(1, NS):
        send(gb.at[s], gb.at[s], 4, shard_peer(i))

    low = lax.broadcasted_iota(jnp.int32, (16, 128), 1) < 64

    def right_block(i, carry):
        block = lax.rem(m // 4 + i, 8)
        columns = pl.ds(pl.multiple_of(block * 256, 256), 256)
        term = jnp.zeros((R, 256), F32)
        for c in range(NX):
            rows = pl.ds(c * CH, CH)
            term += dot(pt[c], gv[rows, columns], ((1,), (0,)))
            term += dot(pt[c], ev[rows, columns], ((1,), (0,)))
        for t in range(2):
            top = term[:16, 128 * t : 128 * t + 128]
            bottom = term[16:, 128 * t : 128 * t + 128]
            for h in range(2):
                p = block * 4 + 2 * t + h
                if h == 0:
                    piece = jnp.where(low, top, pltpu.roll(bottom, 64, 1))
                else:
                    piece = jnp.where(low, pltpu.roll(top, 64, 1), bottom)
                st[p] = piece

                @pl.when(p != m)
                def _():
                    send(st.at[p], rt.at[m], 5, m_device(p))

        return carry

    lax.fori_loop(1, 9, right_block, 0)
    rt[m] = st[m]

    wait_bytes(gb.at[pl.ds(0, NS - 1)], recv_sem.at[4])
    packed = gb[0]
    for k in range(1, NS):
        packed += gb[k]
    gram = jnp.concatenate([packed[:, R * k : R * k + R] for k in range(4)], axis=0)
    inverse = inverse_factor(gram)

    wait_bytes(rt.at[pl.ds(0, NM - 1)], recv_sem.at[5])
    piece = rt[0]
    for k in range(1, NM):
        piece += rt[k]
    tz[z] = piece
    for i in range(1, NZ):
        send(tz.at[z], tz.at[z], 6, z_peer(i))

    for c in range(NX):
        ortho = dot(pt[c].astype(F32), inverse, ((0,), (1,)), HIGHEST)
        high = ortho.astype(BF16)
        rest = (ortho - high.astype(F32)).astype(BF16)
        ohl_ref[pl.ds(c * CH, CH), :] = jnp.concatenate([high, rest], axis=1)

    wait_bytes(tz.at[pl.ds(0, NZ - 1)], recv_sem.at[6])
    piece = tz[0]
    for k in range(1, NZ):
        piece += tz[k]
    term = jnp.concatenate([piece, pltpu.roll(piece, 64, 1)], axis=0)
    right = dot(inverse, term, ((1,), (0,)), HIGHEST) * (1.0 / 32.0)
    qp[m] = jnp.where(low, right[:16], pltpu.roll(right[16:], 64, 1)).astype(BF16)

    def gather(i, carry):
        send(qp.at[m], qp.at[m], 7, m_device(lax.rem(m + i, NM)))
        return carry

    lax.fori_loop(1, NM, gather, 0)

    def merge(i, carry):
        rows = pl.ds(pl.multiple_of(i * 16, 16), 16)
        merged_ref[rows, :] = gv[rows, :].astype(F32) + ev[rows, :].astype(F32)
        return carry

    lax.fori_loop(0, ROWS // 16, merge, 0)
    wait_bytes(qp.at[pl.ds(0, NM - 1)], recv_sem.at[7])
    for t in range(NM // 2):
        first, second = qp[2 * t].astype(F32), qp[2 * t + 1].astype(F32)
        columns = pl.ds(128 * t, 128)
        qn_ref[:16, columns] = jnp.where(low, first, pltpu.roll(second, 64, 1)).astype(BF16)
        qn_ref[16:, columns] = jnp.where(low, pltpu.roll(first, 64, 1), second).astype(BF16)
    mine = qp[replica].astype(F32)
    qsel_ref[:16] = mine.astype(BF16)
    qsel_ref[16:] = pltpu.roll(mine, 64, 1).astype(BF16)

    for ref, at in (
        (qb.at[pl.ds(0, NS - 1)], 0),
        (xr.at[pl.ds(0, NX - 1)], 1),
        (zb.at[pl.ds(0, NZ - 1)], 2),
        (pt.at[pl.ds(0, NX - 1)], 3),
        (gb.at[pl.ds(0, NS - 1)], 4),
        (rt.at[pl.ds(0, NM - 1)], 5),
        (tz.at[pl.ds(0, NZ - 1)], 6),
        (qp.at[pl.ds(0, NM - 1)], 7),
    ):
        wait_bytes(ref, send_sem.at[at])


def residual_kernel(
    merged_ref, ohl_ref, qn_ref, qsel_ref, mom_ref, err_hbm, new_ref, q_ref, staged, sem
):
    s = lax.axis_index("shard")
    q = qn_ref[...]
    q = jnp.concatenate([q, q], axis=0)
    copies = []
    for i in range(ROWS // TILE):
        rows = pl.ds(i * TILE, TILE)
        approx = dot(ohl_ref[rows, :], q, ((1,), (0,)))
        staged[rows, :] = (merged_ref[rows, :] - approx).astype(BF16)
        copies.append(pltpu.make_async_copy(staged.at[rows], err_hbm.at[rows], sem.at[i]))
        copies[-1].start()
    chosen = qsel_ref[...]
    block = dot(jnp.concatenate([chosen, chosen], axis=0), ohl_ref[...], ((0,), (1,)))
    new_ref[...] = 0.9 * mom_ref[...] + block[:64]
    q_ref[...] = qn_ref[:, pl.ds(pl.multiple_of(s * 256, 256), 256)].astype(F32)
    for copy in copies:
        copy.wait()


def shards(grads, errors, q_prev, momentum):
    g = pltpu.with_memory_space_constraint(grads[0], pltpu.HBM)
    e = pltpu.with_memory_space_constraint(errors[0], pltpu.HBM)
    vmem = pl.BlockSpec(memory_space=pltpu.VMEM)
    hbm = pl.BlockSpec(memory_space=pltpu.HBM)
    merged, ohl, qn, qsel = pl.pallas_call(
        exchange_kernel,
        out_shape=(
            pltpu.VMEM((ROWS, COLS), F32),
            jax.ShapeDtypeStruct((ROWS, 2 * R), BF16),
            jax.ShapeDtypeStruct((R, COLS), BF16),
            jax.ShapeDtypeStruct((R, 128), BF16),
        ),
        in_specs=[hbm, hbm, hbm],
        out_specs=(vmem, vmem, vmem, vmem),
        scratch_shapes=[
            pltpu.VMEM((ROWS, COLS), BF16),
            pltpu.VMEM((ROWS, COLS), BF16),
            pltpu.VMEM((NS, R, 256), BF16),
            pltpu.VMEM((NX - 1, R, CH), BF16),
            pltpu.VMEM((NX, R, CH), BF16),
            pltpu.VMEM((NZ, R, CH), BF16),
            pltpu.VMEM((NX, R, CH), BF16),
            pltpu.VMEM((NS, 8, 128), F32),
            pltpu.VMEM((NM, 16, 128), F32),
            pltpu.VMEM((NM, 16, 128), F32),
            pltpu.VMEM((NZ, 16, 128), F32),
            pltpu.VMEM((NM, 16, 128), BF16),
            pltpu.SemaphoreType.DMA((2 * NX + 1,)),
            pltpu.SemaphoreType.DMA((8,)),
            pltpu.SemaphoreType.DMA((8,)),
        ],
        compiler_params=pltpu.CompilerParams(
            collective_id=0, has_side_effects=True, vmem_limit_bytes=40 << 20
        ),
    )(g, e, pltpu.with_memory_space_constraint(q_prev, pltpu.HBM))
    new_errors, new_momentum, q_next = pl.pallas_call(
        residual_kernel,
        out_shape=(
            jax.ShapeDtypeStruct((ROWS, COLS), BF16),
            jax.ShapeDtypeStruct((64, ROWS), F32),
            jax.ShapeDtypeStruct((R, 256), F32),
        ),
        in_specs=[vmem] * 5,
        out_specs=(hbm, vmem, vmem),
        scratch_shapes=[
            pltpu.VMEM((ROWS, COLS), BF16),
            pltpu.SemaphoreType.DMA((ROWS // TILE,)),
        ],
        compiler_params=pltpu.CompilerParams(vmem_limit_bytes=40 << 20),
    )(merged, ohl, qn, qsel, momentum.T)
    return (new_errors[None], new_momentum.T, q_next)


def solution(mesh):
    return jax.shard_map(
        shards,
        mesh=mesh,
        in_specs=(
            P("replica", "shard", None),
            P("replica", "shard", None),
            P(None, "shard"),
            P("shard", "replica"),
        ),
        out_specs=(P("replica", "shard", None), P("shard", "replica"), P(None, "shard")),
        check_vma=False,
    )
```
